32 devices in a mesh: groups: 2 (over y), ep: 4 (over z), tp: 4 (over x, core).
Axes of the slice: x: 2, y: 2, z: 4, core: 2. Of those that a mesh axis runs over, the one named last changes fastest.
Arguments:
- tokens: bfloat16 [1024, 4096], P(('groups', 'ep'), 'tp'), parts along dimension 0, may hold values from -6 to 6
- routes: int32 [1024, 16], P(('groups', 'ep')), parts along dimension 0, may hold values from 0 to 63, all different within a row; in each aligned block of 128 rows (0 to 127, 128 to 255, ...) at most 64 rows name the same one
- gates: float32 [1024, 16], P(('groups', 'ep')), parts along dimension 0, may hold values from 0.02 to 0.12
- w_latent: bfloat16 [4096, 1024], P('tp'), may hold values from -0.09375 to 0.09375
- w_gate: bfloat16 [64, 1024, 2048], P('ep', None, 'tp'), may hold values from -0.1875 to 0.1875
- w_up: bfloat16 [64, 1024, 2048], P('ep', None, 'tp'), may hold values from -0.1875 to 0.1875
- w_out: bfloat16 [64, 2048, 1024], P('ep', 'tp'), may hold values from -0.125 to 0.125
- w_restore: bfloat16 [1024, 4096], P('tp'), may hold values from -0.1875 to 0.1875
Outputs:
- mixed: bfloat16 [1024, 4096], P(('groups', 'ep'), 'tp'), parts along dimension 0
The draws below stay inside these ranges and needn't reach their ends.
There are 2 independent parts, one for each index of `groups`. The reference program is written for one: setup_inputs(seed, part) draws one part's arguments, and reference() takes and returns one part's arrays. A program takes and returns all parts, laid end to end along the dimension named above; an argument that names none is the same for every part. Nothing has to cross between parts.
Inputs may be any that keep to these rules, and one draw needn't show every extreme that they name: `routes`: each row names 16 different experts. Within the rows of one device (aligned blocks of 128 rows) no expert is named by more than 64 rows, a bound that some block reaches.
All inputs are finite; a program needn't handle non-finite values.
Results may differ from the reference program's by a relative error of at most 0.025.
Values may be sent and summed in bfloat16 or wider, within the bound.
A program may use at most 192 MiB of HBM per device.

```python
import math
import jax
import jax.numpy as jnp
import numpy as np
from jax import lax

D = 4096
L = 1024
FF = 2048
TOP = 16
EXPERTS = 64
TOK_DEV = 128
CAP = 64
TOKENS = 512
N_EP = 4
N_TP = 4


def levels(rng, extent, shards, low, top_value):
    def one(dim, blocks):
        steps = jax.random.uniform(jax.random.fold_in(jax.random.fold_in(rng, 6), dim), (blocks,), jnp.float32, low / len(shards), top_value / len(shards))
        return jnp.repeat(jnp.exp(steps), extent[dim] // blocks).reshape((-1,) + (1,) * (len(extent) - dim - 1))

    factor_of = one(*shards[0])
    for cut in shards[1:]:
        factor_of = factor_of * one(*cut)
    return factor_of


def deal_out(own_key, own, number, rows, count, top, reach, lean):
    order = jax.random.permutation(own_key, count)
    heavy_load, usual = portions_of(count, rows * top, reach, lean, True), portions_of(count, rows * top, reach, lean, False)
    places = jnp.arange(count)

    def named(lengths, offset_by):
        used = int((lengths > 0).sum())
        fixed = max(1, used // 4)
        moved = fixed + (places - fixed + offset_by * (used - fixed)) % max(1, count - fixed)
        return jnp.zeros((count,), jnp.int32).at[order[jnp.where(places < fixed, places, moved)]].set(jnp.asarray(lengths, jnp.int32))

    lengths = jnp.where(number % 4 == 0, named(heavy_load, number // 4), named(usual, number - number // 4 - 1))
    mixed = jax.random.permutation(jax.random.fold_in(own, 3), count)
    source_of, sink = mixed[0:count // 2 * 2:2], mixed[1:count // 2 * 2:2]
    room = jnp.minimum(lengths[source_of] - 1, reach - lengths[sink]) // 2
    room = jnp.where((source_of == order[0]) | (sink == order[0]) | (lengths[sink] == 0), 0, jnp.maximum(room, 0))
    moved = jax.random.randint(jax.random.fold_in(own, 4), (count // 2,), 0, 1 << 20) % (room + 1)
    lengths = lengths.at[source_of].add(-moved).at[sink].add(moved)
    items = jnp.searchsorted(jnp.cumsum(lengths), jnp.arange(rows * top), side="right").astype(jnp.int32)
    listing = items.reshape(top, rows).T
    listing = listing[jax.random.permutation(jax.random.fold_in(own, 1), rows)]
    offset_by = jax.random.randint(jax.random.fold_in(own, 2), (rows, 1), 0, top)
    return jnp.take_along_axis(listing, (jnp.arange(top)[None, :] + offset_by) % top, axis=1)


def portions_of(amount, total, limit, skew, full):
    portions = [(1 << 20) // math.isqrt(standing ** skew) + 1 for standing in range(1, amount + 1)]
    largest = limit if full else min(limit, max(-(-total // amount), total * portions[0] // sum(portions)))
    least = 1 if total - largest >= amount - 1 else 0
    given, spare = [largest] + [least] * (amount - 1), total - largest - least * (amount - 1)
    while spare > 0:
        candidates = [i for i in range(1, amount) if given[i] < largest] or [i for i in range(1, amount) if given[i] < limit]
        pool, left = sum([portions[i] for i in candidates]), spare
        for i in candidates:
            extra = min(limit - given[i], max(1, left * portions[i] // pool), spare)
            given[i] = given[i] + extra
            spare = spare - extra
    return np.array(given)


def centred(key, shape, width, most, pieces=(), held_as=jnp.bfloat16):
    drawn = width * jax.random.normal(key, shape, jnp.float32)
    if pieces:
        drawn = drawn * levels(key, shape, pieces, -0.22, 0.18)
    return jnp.clip(drawn, -most, most).astype(held_as)


def setup_inputs(seed: int = 0, part: int = 0) -> dict:
    streams_of = jax.random.split(jax.random.key(seed), 9)
    own_keys = jax.random.split(jax.random.fold_in(streams_of[8], part), 9)
    tokens = centred(own_keys[0], (TOKENS, D), 1.0, 6.0, ((0, 4), (1, 4)))
    routes_keys = jax.random.split(jax.random.fold_in(own_keys[1], 1), TOKENS // TOK_DEV)
    routes_turns = jax.random.permutation(jax.random.fold_in(own_keys[1], 3), TOKENS // TOK_DEV)
    routes = jax.vmap(lambda own, number: deal_out(jax.random.fold_in(own_keys[1], 2), own, number, TOK_DEV, EXPERTS, TOP, CAP, 2))(routes_keys, routes_turns).reshape((TOKENS, TOP))
    gates = jnp.clip(0.02 + 0.09999999776482582 * jax.random.uniform(own_keys[2], (TOKENS, TOP), jnp.float32) ** levels(own_keys[2], (TOKENS, TOP), ((0, 4),), -0.2, 0.2), 0.02, 0.12)
    w_latent = centred(streams_of[3], (D, L), D ** -0.5, 0.09375, ((0, 4),))
    w_gate = centred(streams_of[4], (EXPERTS, L, FF), L ** -0.5, 0.1875, ((0, 4), (2, 4)))
    w_up = centred(streams_of[5], (EXPERTS, L, FF), L ** -0.5, 0.1875, ((0, 4), (2, 4)))
    w_out = centred(streams_of[6], (EXPERTS, FF, L), FF ** -0.5, 0.125, ((0, 4), (1, 4)))
    w_restore = centred(streams_of[7], (L, D), L ** -0.5, 0.1875, ((0, 4),))
    return {"tokens": tokens, "routes": routes, "gates": gates, "w_latent": w_latent, "w_gate": w_gate, "w_up": w_up, "w_out": w_out, "w_restore": w_restore}


def reference(tokens, routes, gates, w_latent, w_gate, w_up, w_out, w_restore):
    latent = jnp.dot(tokens, w_latent, preferred_element_type=jnp.float32).astype(jnp.bfloat16)
    blocks = routes.reshape(N_EP, TOK_DEV * TOP)
    onehot = (blocks[:, :, None] == jnp.arange(EXPERTS, dtype=jnp.int32)[None, None, :]).astype(jnp.int32)
    before = jnp.cumsum(onehot, axis=1) - onehot
    ranks = jnp.sum(before * onehot, axis=2)
    source = jnp.arange(N_EP, dtype=jnp.int32)[:, None]
    pair_ids = jnp.arange(TOK_DEV * TOP, dtype=jnp.int32)[None, :]
    slot = (source * CAP + ranks).reshape(-1).astype(jnp.int32)
    token_ids = (source * TOK_DEV + pair_ids // TOP).reshape(-1).astype(jnp.int32)
    expert_ids = blocks.reshape(-1).astype(jnp.int32)
    table = jnp.full((EXPERTS, N_EP * CAP), TOKENS, jnp.int32).at[expert_ids, slot].set(token_ids)
    weights = jnp.zeros((EXPERTS, N_EP * CAP), jnp.float32).at[expert_ids, slot].set(gates.reshape(-1))
    padded = jnp.concatenate([latent, jnp.zeros((1, L), jnp.bfloat16)], axis=0)
    group = FF // N_TP

    def one_expert(carry, expert):
        index = table[expert]
        rows = padded[index]
        gate = jnp.dot(rows, w_gate[expert], preferred_element_type=jnp.float32)
        upper = jnp.dot(rows, w_up[expert], preferred_element_type=jnp.float32)
        hidden = (jax.nn.silu(gate) * upper).astype(jnp.bfloat16)
        outer = w_out[expert]
        total = jnp.zeros((N_EP * CAP, L), jnp.float32)
        for part_index in range(N_TP):
            piece = jnp.dot(hidden[:, part_index * group:(part_index + 1) * group],
                            outer[part_index * group:(part_index + 1) * group],
                            preferred_element_type=jnp.float32)
            total = total + piece.astype(jnp.bfloat16).astype(jnp.float32)
        result = total.astype(jnp.bfloat16).astype(jnp.float32)
        carry = carry.at[index].add(weights[expert][:, None] * result)
        return carry, None

    start = jnp.zeros((TOKENS + 1, L), jnp.float32)
    summed, _ = lax.scan(one_expert, start, jnp.arange(EXPERTS, dtype=jnp.int32))
    combined = summed[:TOKENS].astype(jnp.bfloat16)
    return jnp.dot(combined, w_restore, preferred_element_type=jnp.float32).astype(jnp.bfloat16)
```

```python
import jax
import jax.numpy as jnp
from jax import lax
from jax.experimental import pallas as pl
from jax.experimental.pallas import tpu as pltpu
from jax.sharding import PartitionSpec as P


def ffn_kernel(lat_ref, routes_ref, gates_ref, ids_ref, wg_ref, wu_ref, wo_ref, out_ref, acc_ref):
    step = pl.program_id(0)
    count = pl.num_programs(0)
    rows = lat_ref.shape[0]
    tile = min(rows, 256)
    expert = ids_ref[0] + step

    @pl.when(step == 0)
    def _():
        acc_ref[...] = jnp.zeros_like(acc_ref)

    def body(i, carry):
        r = pl.ds(pl.multiple_of(i * tile, tile), tile)
        x = lat_ref[r, :]
        weight = jnp.sum(jnp.where(routes_ref[r, :] == expert, gates_ref[r, :], 0.0), axis=1, keepdims=True)
        g = jnp.dot(x, wg_ref[0], preferred_element_type=jnp.float32)
        u = jnp.dot(x, wu_ref[0], preferred_element_type=jnp.float32)
        h = (g / (1.0 + jnp.exp(-g)) * u * weight).astype(jnp.bfloat16)
        acc_ref[r, :] += jnp.dot(h, wo_ref[0], preferred_element_type=jnp.float32)
        return carry

    lax.fori_loop(0, rows // tile, body, 0)

    @pl.when(step == count - 1)
    def _():
        out_ref[...] = acc_ref[...].astype(out_ref.dtype)


def ffn(lat, routes, gates, first, wg, wu, wo):
    rows, width = lat.shape
    count, _, hidden = wg.shape
    top = routes.shape[1]
    whole = lambda *shape: pl.BlockSpec(shape, lambda e: (0,) * len(shape))
    return pl.pallas_call(
        ffn_kernel,
        grid=(count,),
        out_shape=jax.ShapeDtypeStruct((rows, width), jnp.bfloat16),
        in_specs=[
            whole(rows, width),
            whole(rows, top),
            whole(rows, top),
            pl.BlockSpec(memory_space=pltpu.SMEM),
            pl.BlockSpec((1, width, hidden), lambda e: (e, 0, 0)),
            pl.BlockSpec((1, width, hidden), lambda e: (e, 0, 0)),
            pl.BlockSpec((1, hidden, width), lambda e: (e, 0, 0)),
        ],
        out_specs=whole(rows, width),
        scratch_shapes=[pltpu.VMEM((rows, width), jnp.float32)],
        compiler_params=pltpu.CompilerParams(vmem_limit_bytes=56 * 1024 * 1024),
    )(lat, routes, gates, first, wg, wu, wo)


def shards(tokens, routes, gates, w_latent, w_gate, w_up, w_out, w_restore):
    count = w_gate.shape[0]
    partial_value = jnp.dot(tokens, w_latent, preferred_element_type=jnp.float32)
    routes_all = lax.all_gather(routes, "ep", axis=0, tiled=True)
    gates_all = lax.all_gather(gates, "ep", axis=0, tiled=True)
    latent_part = lax.psum_scatter(
        partial_value.astype(jnp.bfloat16), "tp", scatter_dimension=1, tiled=True
    )
    lat = lax.all_gather(latent_part, "ep", axis=0, tiled=True)
    lat = lax.all_gather(lat, "tp", axis=1, tiled=True)
    first = (lax.axis_index("ep") * count).astype(jnp.int32).reshape(1)
    part = ffn(lat, routes_all, gates_all, first, w_gate, w_up, w_out)
    part = lax.psum_scatter(part, "tp", scatter_dimension=1, tiled=True)
    combined = lax.psum_scatter(part, "ep", scatter_dimension=0, tiled=True)
    restored = jnp.dot(combined, w_restore, preferred_element_type=jnp.float32)
    return lax.psum_scatter(restored.astype(jnp.bfloat16), "tp", scatter_dimension=1, tiled=True)


def solution(mesh):
    return jax.shard_map(
        shards,
        mesh=mesh,
        in_specs=(
            P(("groups", "ep"), "tp"),
            P(("groups", "ep"), None),
            P(("groups", "ep"), None),
            P("tp", None),
            P("ep", None, "tp"),
            P("ep", None, "tp"),
            P("ep", "tp", None),
            P("tp", None),
        ),
        out_specs=P(("groups", "ep"), "tp"),
        check_vma=False,
    )
```

```python
import functools

import jax
import jax.numpy as jnp
from jax import lax
from jax.experimental import pallas as pl
from jax.experimental.pallas import tpu as pltpu
from jax.sharding import PartitionSpec as P

F32, BF16 = jnp.float32, jnp.bfloat16
MESH = pl.DeviceIdType.MESH
SLOTS = 4


def remote(src, dst, send, recv, **where):
    return pltpu.make_async_remote_copy(
        src_ref=src, dst_ref=dst, send_sem=send, recv_sem=recv, device_id=where, device_id_type=MESH
    )


def layer(
    ep_n, tp_n, tok_ref, pack_ref, wl_ref, wg_hbm, wu_hbm, wo_hbm, wr_hbm, out_ref,
    p_send, p_recv, lat, pack, wg, wu, wo, wr, acc, r1_send, r1_recv, r2_send, r2_recv,
    r3_send, r3_recv, comb,
    p_sems, k_sems, a_sems, b1_sems, b2_sems, b3_sems, w_sems, wr_sems, own_sem,
    r1_sems, r2_sems, r3_sems, c_sems,
):
    ep, tp = lax.axis_index("ep"), lax.axis_index("tp")
    far = lax.rem(tp + 2, 4)
    near = tp + 1 - 2 * lax.rem(tp, 2)
    near_far = lax.rem(near + 2, 4)
    count = wg_hbm.shape[0]
    slots = wg.shape[0]
    toks, top = tok_ref.shape[0], pack_ref.shape[1] // 2
    rows, width = lat.shape
    quarter = width // tp_n
    out_cols = out_ref.shape[1]

    def cols(q):
        return pl.ds(pl.multiple_of(q * quarter, quarter), quarter)

    def block(b):
        return pl.ds(pl.multiple_of(b * toks, toks), toks)

    def loads(e, s):
        return [
            pltpu.make_async_copy(hbm.at[e], vmem.at[s], w_sems.at[s, i])
            for i, (hbm, vmem) in enumerate(((wg_hbm, wg), (wu_hbm, wu), (wo_hbm, wo)))
        ]

    for s in range(slots):
        for c in loads(s, s):
            c.start()

    barrier = pltpu.get_barrier_semaphore()
    for d in range(1, ep_n):
        pl.semaphore_signal(barrier, inc=1, device_id={"ep": lax.rem(ep + d, ep_n)}, device_id_type=MESH)
    for d in range(1, tp_n):
        pl.semaphore_signal(barrier, inc=1, device_id={"tp": lax.rem(tp + d, tp_n)}, device_id_type=MESH)
    pl.semaphore_wait(barrier, ep_n + tp_n - 2)

    sent = []

    parts = [None]
    for d in range(1, tp_n):
        peer = lax.rem(tp + d, tp_n)
        p_send[d] = jnp.dot(tok_ref[...], wl_ref[:, cols(peer)], preferred_element_type=F32).astype(BF16)
        c = remote(p_send.at[d], p_recv.at[d], p_sems.at[0, d], p_sems.at[1, d], tp=peer)
        c.start()
        parts.append(c)
        sent.append(c)
    mine = jnp.dot(tok_ref[...], wl_ref[:, cols(tp)], preferred_element_type=F32)
    packs = [None]
    pack[block(ep), :] = pack_ref[...]
    for d in range(1, ep_n):
        c = remote(
            pack_ref, pack.at[block(ep), :], k_sems.at[0, d], k_sems.at[1, d], ep=lax.rem(ep + d, ep_n)
        )
        c.start()
        packs.append(c)
        sent.append(c)
    for d in range(1, tp_n):
        parts[d].wait_recv()
        mine = mine + p_recv[d].astype(F32)
    lat[block(ep), cols(tp)] = mine.astype(BF16)

    own = lat.at[block(ep), cols(tp)]
    spread = [None]
    for d in range(1, ep_n):
        c = remote(own, own, a_sems.at[0, d], a_sems.at[1, d], ep=lax.rem(ep + d, ep_n))
        c.start()
        spread.append(c)
        sent.append(c)
    b1, b2, b3 = [], [], []
    for d in range(ep_n):
        if d:
            spread[d].wait_recv()
        piece = lat.at[block(lax.rem(ep + ep_n - d, ep_n)), cols(tp)]
        c = remote(piece, piece, b1_sems.at[0, d], b1_sems.at[1, d], tp=far)
        c.start()
        b1.append(c)
        c = remote(piece, piece, b2_sems.at[0, d], b2_sems.at[1, d], tp=near)
        c.start()
        b2.append(c)
    for d in range(ep_n):
        b1[d].wait_recv()
        piece = lat.at[block(lax.rem(ep + ep_n - d, ep_n)), cols(far)]
        c = remote(piece, piece, b3_sems.at[0, d], b3_sems.at[1, d], tp=near)
        c.start()
        b3.append(c)
    sent += b1 + b2 + b3
    for d in range(ep_n):
        b2[d].wait_recv()
        b3[d].wait_recv()
        if d:
            packs[d].wait_recv()

    restore = []
    for d in range(1, tp_n):
        peer = lax.rem(tp + d, tp_n)
        c = remote(
            wr_hbm.at[:, pl.ds(pl.multiple_of(peer * out_cols, out_cols), out_cols)],
            wr.at[cols(tp), :], wr_sems.at[0, d], wr_sems.at[1, d], tp=peer,
        )
        c.start()
        restore.append(c)
        sent.append(c)
    own_restore = pltpu.make_async_copy(
        wr_hbm.at[:, pl.ds(pl.multiple_of(tp * out_cols, out_cols), out_cols)], wr.at[cols(tp), :], own_sem
    )
    own_restore.start()

    acc[...] = jnp.zeros_like(acc)
    tile = min(rows, 256)
    pair = min(rows // tile, 2)

    def expert(e, carry):
        s = lax.rem(e, slots)
        for c in loads(e, s):
            c.wait()
        name = (ep * count + e).astype(F32)

        def tiles(i, inner):
            for j in range(pair):
                r = pl.ds(pl.multiple_of((i * pair + j) * tile, tile), tile)
                x = lat[r, :]
                chosen = pack[r, :]
                weight = jnp.sum(
                    jnp.where(chosen[:, :top] == name, chosen[:, top:], 0.0), axis=1, keepdims=True
                )
                g = jnp.dot(x, wg[s], preferred_element_type=F32)
                u = jnp.dot(x, wu[s], preferred_element_type=F32)
                h = (g / (1.0 + jnp.exp(-g)) * u * weight).astype(BF16)
                acc[r, :] += jnp.dot(h, wo[s], preferred_element_type=F32)
            return inner

        if rows == tile * pair:
            tiles(0, 0)
        else:
            lax.fori_loop(0, rows // (tile * pair), tiles, 0)

        @pl.when(e + slots < count)
        def _():
            for c in loads(e + slots, s):
                c.start()

        return carry

    lax.fori_loop(0, count, expert, 0)

    order = list(range(1, ep_n)) + [0]
    at = [block(lax.rem(ep + d, ep_n)) for d in range(ep_n)]
    r1, r2, r3 = {}, {}, {}
    for d in order:
        r1_send[d, 0] = acc[at[d], cols(near)].astype(BF16)
        r1_send[d, 1] = acc[at[d], cols(near_far)].astype(BF16)
        r1[d] = remote(r1_send.at[d], r1_recv.at[d], r1_sems.at[0, d], r1_sems.at[1, d], tp=near)
        r1[d].start()
    for d in order:
        r1[d].wait_recv()
        r2_send[d] = (acc[at[d], cols(far)] + r1_recv[d, 1].astype(F32)).astype(BF16)
        r2[d] = remote(r2_send.at[d], r2_recv.at[d], r2_sems.at[0, d], r2_sems.at[1, d], tp=far)
        r2[d].start()
    for d in order:
        r2[d].wait_recv()
        total = acc[at[d], cols(tp)] + r1_recv[d, 0].astype(F32) + r2_recv[d].astype(F32)
        if d:
            r3_send[d] = total.astype(BF16)
            r3[d] = remote(
                r3_send.at[d], r3_recv.at[d], r3_sems.at[0, d], r3_sems.at[1, d], ep=lax.rem(ep + d, ep_n)
            )
            r3[d].start()
    for d in range(1, ep_n):
        r3[d].wait_recv()
        total = total + r3_recv[d].astype(F32)
    sent += list(r1.values()) + list(r2.values()) + list(r3.values())
    comb[:, cols(tp)] = total.astype(BF16)
    gathered = []
    for d in range(1, tp_n):
        c = remote(
            comb.at[:, cols(tp)], comb.at[:, cols(tp)], c_sems.at[0, d], c_sems.at[1, d],
            tp=lax.rem(tp + d, tp_n),
        )
        c.start()
        gathered.append(c)
    sent += gathered
    own_restore.wait()
    for c in restore:
        c.wait_recv()
    for c in gathered:
        c.wait_recv()
    out_ref[...] = jnp.dot(comb[...], wr[...], preferred_element_type=F32).astype(out_ref.dtype)
    for c in sent:
        c.wait_send()


def solution(mesh):
    ep_n, tp_n = mesh.shape["ep"], mesh.shape["tp"]

    def shards(tokens, routes, gates, w_latent, w_gate, w_up, w_out, w_restore):
        toks = tokens.shape[0]
        count, width, hidden = w_gate.shape
        rows, quarter = toks * ep_n, width // tp_n
        out_cols = w_restore.shape[1] // tp_n
        slots = min(SLOTS, count)
        pack = jnp.concatenate([routes.astype(F32), gates], axis=1)
        vmem, dma = pltpu.VMEM, pltpu.SemaphoreType.DMA
        in_vmem, in_hbm = pl.BlockSpec(memory_space=pltpu.VMEM), pl.BlockSpec(memory_space=pl.ANY)
        work = 6 * rows * width * hidden * count
        return pl.pallas_call(
            functools.partial(layer, ep_n, tp_n),
            out_shape=jax.ShapeDtypeStruct((toks, out_cols), BF16),
            in_specs=[in_vmem] * 3 + [in_hbm] * 4,
            out_specs=in_vmem,
            scratch_shapes=[
                vmem((tp_n, toks, quarter), BF16),
                vmem((tp_n, toks, quarter), BF16),
                vmem((rows, width), BF16),
                vmem((rows, pack.shape[1]), F32),
                vmem((slots, width, hidden), BF16),
                vmem((slots, width, hidden), BF16),
                vmem((slots, hidden, width), BF16),
                vmem((width, out_cols), BF16),
                vmem((rows, width), F32),
                vmem((ep_n, 2, toks, quarter), BF16),
                vmem((ep_n, 2, toks, quarter), BF16),
                vmem((ep_n, toks, quarter), BF16),
                vmem((ep_n, toks, quarter), BF16),
                vmem((ep_n, toks, quarter), BF16),
                vmem((ep_n, toks, quarter), BF16),
                vmem((toks, width), BF16),
                dma((2, tp_n)),
                dma((2, ep_n)),
                dma((2, ep_n)),
                dma((2, ep_n)),
                dma((2, ep_n)),
                dma((2, ep_n)),
                dma((slots, 3)),
                dma((2, tp_n)),
                dma,
                dma((2, ep_n)),
                dma((2, ep_n)),
                dma((2, ep_n)),
                dma((2, tp_n)),
            ],
            compiler_params=pltpu.CompilerParams(
                collective_id=0, has_side_effects=True, vmem_limit_bytes=60 * 1024 * 1024
            ),
            cost_estimate=pl.CostEstimate(flops=work, bytes_accessed=6 * width * hidden * count, transcendentals=0),
        )(tokens, pack, w_latent, w_gate, w_up, w_out, w_restore)

    return jax.shard_map(
        shards,
        mesh=mesh,
        in_specs=(
            P(("groups", "ep"), "tp"),
            P(("groups", "ep"), None),
            P(("groups", "ep"), None),
            P("tp", None),
            P("ep", None, "tp"),
            P("ep", None, "tp"),
            P("ep", "tp", None),
            P("tp", None),
        ),
        out_specs=P(("groups", "ep"), "tp"),
        check_vma=False,
    )
```

```python
import functools

import jax
import jax.numpy as jnp
from jax import lax
from jax.experimental import pallas as pl
from jax.experimental.pallas import tpu as pltpu
from jax.sharding import PartitionSpec as P

F32, BF16 = jnp.float32, jnp.bfloat16
MESH = pl.DeviceIdType.MESH
SLOTS = 12


def remote(src, dst, send, recv, **where):
    return pltpu.make_async_remote_copy(
        src_ref=src, dst_ref=dst, send_sem=send, recv_sem=recv, device_id=where, device_id_type=MESH
    )


def layer(
    ep_n, tp_n, tok_ref, pack_ref, wl_ref, wg_hbm, wu_hbm, wo_hbm, wr_hbm, out_ref,
    p_send, p_recv, lat, pack, wg, wu, wo, wr, acc, r1_send, r1_recv, r2_send, r2_recv,
    r3_send, r3_recv, comb,
    p_sems, k_sems, a_sems, b1_sems, b2_sems, b3_sems, w_sems, wr_sems, own_sem,
    r1_sems, r2_sems, r3_sems, c_sems,
):
    ep, tp = lax.axis_index("ep"), lax.axis_index("tp")
    far = lax.rem(tp + 2, 4)
    near = tp + 1 - 2 * lax.rem(tp, 2)
    near_far = lax.rem(near + 2, 4)
    count = wg_hbm.shape[0]
    toks, top = tok_ref.shape[0], pack_ref.shape[1] // 2
    rows, width = lat.shape
    quarter = width // tp_n
    out_cols = out_ref.shape[1]
    unit = 2 if count % 2 == 0 else 1
    groups, held = count // unit, wg.shape[0] // unit
    half = ep_n // 2

    def cols(q):
        return pl.ds(pl.multiple_of(q * quarter, quarter), quarter)

    def block(d):
        return pl.ds(d * toks, toks)

    def after(d):
        return lax.rem(ep + d, ep_n)

    def loads(q):
        s = lax.rem(q, held) * unit
        return [
            pltpu.make_async_copy(hbm.at[q * unit + j], vmem.at[s + j], w_sems.at[s + j, i])
            for j in range(unit)
            for i, (hbm, vmem) in enumerate(((wg_hbm, wg), (wu_hbm, wu), (wo_hbm, wo)))
        ]

    def begin(q):
        for c in loads(q):
            c.start()

    early = min(held, 2)
    for q in range(early):
        begin(q)

    barrier = pltpu.get_barrier_semaphore()
    for d in range(1, ep_n):
        pl.semaphore_signal(barrier, inc=1, device_id={"ep": after(d)}, device_id_type=MESH)
    for d in range(1, tp_n):
        pl.semaphore_signal(barrier, inc=1, device_id={"tp": lax.rem(tp + d, tp_n)}, device_id_type=MESH)
    acc[...] = jnp.zeros_like(acc)
    pack[block(0), :] = pack_ref[...]
    pl.semaphore_wait(barrier, ep_n + tp_n - 2)

    def part(d):
        return remote(p_send.at[d], p_recv.at[d], p_sems.at[0, d], p_sems.at[1, d], tp=lax.rem(tp + d, tp_n))

    def packs(d):
        return remote(pack_ref, pack.at[block(d), :], k_sems.at[0, d], k_sems.at[1, d], ep=after(d))

    def spread(d):
        return remote(
            lat.at[block(0), cols(tp)], lat.at[block(d), cols(tp)], a_sems.at[0, d], a_sems.at[1, d], ep=after(d)
        )

    def b1(d):
        piece = lat.at[block(d), cols(tp)]
        return remote(piece, piece, b1_sems.at[0, d], b1_sems.at[1, d], tp=far)

    def b2(d):
        piece = lat.at[block(d), cols(tp)]
        return remote(piece, piece, b2_sems.at[0, d], b2_sems.at[1, d], tp=near)

    def b3(d):
        piece = lat.at[block(d), cols(far)]
        return remote(piece, piece, b3_sems.at[0, d], b3_sems.at[1, d], tp=near)

    def restore(d):
        peer = lax.rem(tp + d, tp_n)
        return remote(
            wr_hbm.at[:, pl.ds(pl.multiple_of(peer * out_cols, out_cols), out_cols)],
            wr.at[cols(tp), :], wr_sems.at[0, d], wr_sems.at[1, d], tp=peer,
        )

    own_restore = pltpu.make_async_copy(
        wr_hbm.at[:, pl.ds(pl.multiple_of(tp * out_cols, out_cols), out_cols)], wr.at[cols(tp), :], own_sem
    )

    def r1(d):
        return remote(r1_send.at[d], r1_recv.at[d], r1_sems.at[0, d], r1_sems.at[1, d], tp=near)

    def r2(d):
        return remote(r2_send.at[d], r2_recv.at[d], r2_sems.at[0, d], r2_sems.at[1, d], tp=far)

    def r3(d):
        return remote(r3_send.at[d], r3_recv.at[d], r3_sems.at[0, d], r3_sems.at[1, d], ep=after(ep_n - d))

    def gathered(d):
        piece = comb.at[:, cols(tp)]
        return remote(piece, piece, c_sems.at[0, d], c_sems.at[1, d], tp=lax.rem(tp + d, tp_n))

    first, second = list(range(half)), list(range(half, ep_n))

    for d in range(1, tp_n):
        w = wl_ref[:, cols(lax.rem(tp + d, tp_n))]
        p_send[d] = jnp.dot(tok_ref[...], w, preferred_element_type=F32).astype(BF16)
        part(d).start()
    mine = jnp.dot(tok_ref[...], wl_ref[:, cols(tp)], preferred_element_type=F32)
    for d in range(1, ep_n):
        packs(d).start()
    for d in range(1, tp_n):
        part(d).wait_recv()
        mine = mine + p_recv[d].astype(F32)
    lat[block(0), cols(tp)] = mine.astype(BF16)

    for d in range(1, ep_n):
        spread(d).start()

    def across(blocks):
        for d in blocks:
            if d:
                spread(d).wait_recv()
            b1(d).start()
            b2(d).start()

    def onward(blocks):
        for d in blocks:
            b1(d).wait_recv()
            b3(d).start()

    def arrived(blocks):
        for d in blocks:
            b2(d).wait_recv()
            b3(d).wait_recv()
            if d:
                packs(d).wait_recv()

    def sum_near(blocks):
        for d in blocks:
            r1_send[d, 0] = acc[block(d), cols(near)].astype(BF16)
            r1_send[d, 1] = acc[block(d), cols(near_far)].astype(BF16)
            r1(d).start()

    def sum_far(blocks):
        for d in blocks:
            r1(d).wait_recv()
            r2_send[d] = (acc[block(d), cols(far)] + r1_recv[d, 1].astype(F32)).astype(BF16)
            r2(d).start()

    def sum_ep(blocks):
        for d in blocks:
            r2(d).wait_recv()
            total = acc[block(d), cols(tp)] + r1_recv[d, 0].astype(F32) + r2_recv[d].astype(F32)
            if d:
                r3_send[d] = total.astype(BF16)
                r3(d).start()
            else:
                acc[block(d), cols(tp)] = total

    def exchange():
        for d in range(1, tp_n):
            restore(d).start()
        own_restore.start()

    across(first)
    for q in range(early, held):
        begin(q)
    onward(first)
    arrived(first)

    span = half * toks
    tile = min(span, 256)

    def experts(p, carry):
        back = p >= groups
        q = jnp.where(back, 2 * groups - 1 - p, p)
        base = jnp.where(back, span, 0)
        s = lax.rem(q, held) * unit

        @pl.when(jnp.logical_or(p < groups, q < groups - held))
        def _():
            for c in loads(q):
                c.wait()

        def tiles(i, inner):
            r = pl.ds(pl.multiple_of(base + i * tile, tile), tile)
            x = lat[r, :]
            chosen = pack[r, :]
            names, weights = chosen[:, :top], chosen[:, top:]
            hs = []
            for j in range(unit):
                name = (ep * count + q * unit + j).astype(F32)
                weight = jnp.sum(jnp.where(names == name, weights, 0.0), axis=1, keepdims=True)
                g = jnp.dot(x, wg[s + j], preferred_element_type=F32)
                u = jnp.dot(x, wu[s + j], preferred_element_type=F32)
                hs.append((g / (1.0 + jnp.exp(-g)) * u * weight).astype(BF16))
            total = acc[r, :]
            for j in range(unit):
                total = total + jnp.dot(hs[j], wo[s + j], preferred_element_type=F32)
            acc[r, :] = total
            return inner

        if span == tile:
            tiles(0, 0)
        else:
            lax.fori_loop(0, span // tile, tiles, 0)

        @pl.when(jnp.logical_and(p < groups, q + held < groups))
        def _():
            begin(q + held)

        @pl.when(jnp.logical_and(p >= groups, q >= held))
        def _():
            begin(q - held)

        last = groups - 1
        for when, what in (
            (0, lambda: across(second)),
            (min(1, last), lambda: onward(second)),
            (min(3, last), exchange),
            (last, lambda: arrived(second)),
            (last, lambda: sum_near(first)),
            (groups + min(1, last), lambda: sum_far(first)),
            (groups + min(3, last), lambda: sum_ep(first)),
        ):
            pl.when(p == when)(what)
        return carry

    lax.fori_loop(0, 2 * groups, experts, 0)

    sum_near(second)
    sum_far(second)
    sum_ep(second)
    total = acc[block(0), cols(tp)]
    for d in range(1, ep_n):
        r3(d).wait_recv()
        total = total + r3_recv[d].astype(F32)
    comb[:, cols(tp)] = total.astype(BF16)
    for d in range(1, tp_n):
        gathered(d).start()
    own_restore.wait()
    for d in range(1, tp_n):
        restore(d).wait_recv()
    for d in range(1, tp_n):
        gathered(d).wait_recv()
    out_ref[...] = jnp.dot(comb[...], wr[...], preferred_element_type=F32).astype(out_ref.dtype)
    for d in range(ep_n):
        for c in (b1, b2, b3, r1, r2):
            c(d).wait_send()
        if d:
            for c in (packs, spread, r3):
                c(d).wait_send()
    for d in range(1, tp_n):
        for c in (part, restore, gathered):
            c(d).wait_send()


def solution(mesh):
    ep_n, tp_n = mesh.shape["ep"], mesh.shape["tp"]

    def shards(tokens, routes, gates, w_latent, w_gate, w_up, w_out, w_restore):
        toks = tokens.shape[0]
        count, width, hidden = w_gate.shape
        rows, quarter = toks * ep_n, width // tp_n
        out_cols = w_restore.shape[1] // tp_n
        slots = min(SLOTS, count)
        pack = jnp.concatenate([routes.astype(F32), gates], axis=1)
        vmem, dma = pltpu.VMEM, pltpu.SemaphoreType.DMA
        in_vmem, in_hbm = pl.BlockSpec(memory_space=pltpu.VMEM), pl.BlockSpec(memory_space=pl.ANY)
        work = 6 * rows * width * hidden * count
        return pl.pallas_call(
            functools.partial(layer, ep_n, tp_n),
            out_shape=jax.ShapeDtypeStruct((toks, out_cols), BF16),
            in_specs=[in_vmem] * 3 + [in_hbm] * 4,
            out_specs=in_vmem,
            scratch_shapes=[
                vmem((tp_n, toks, quarter), BF16),
                vmem((tp_n, toks, quarter), BF16),
                vmem((rows, width), BF16),
                vmem((rows, pack.shape[1]), F32),
                vmem((slots, width, hidden), BF16),
                vmem((slots, width, hidden), BF16),
                vmem((slots, hidden, width), BF16),
                vmem((width, out_cols), BF16),
                vmem((rows, width), F32),
                vmem((ep_n, 2, toks, quarter), BF16),
                vmem((ep_n, 2, toks, quarter), BF16),
                vmem((ep_n, toks, quarter), BF16),
                vmem((ep_n, toks, quarter), BF16),
                vmem((ep_n, toks, quarter), BF16),
                vmem((ep_n, toks, quarter), BF16),
                vmem((toks, width), BF16),
                dma((2, tp_n)),
                dma((2, ep_n)),
                dma((2, ep_n)),
                dma((2, ep_n)),
                dma((2, ep_n)),
                dma((2, ep_n)),
                dma((slots, 3)),
                dma((2, tp_n)),
                dma,
                dma((2, ep_n)),
                dma((2, ep_n)),
                dma((2, ep_n)),
                dma((2, tp_n)),
            ],
            compiler_params=pltpu.CompilerParams(
                collective_id=0, has_side_effects=True, vmem_limit_bytes=60 * 1024 * 1024
            ),
            cost_estimate=pl.CostEstimate(flops=work, bytes_accessed=6 * width * hidden * count, transcendentals=0),
        )(tokens, pack, w_latent, w_gate, w_up, w_out, w_restore)

    return jax.shard_map(
        shards,
        mesh=mesh,
        in_specs=(
            P(("groups", "ep"), "tp"),
            P(("groups", "ep"), None),
            P(("groups", "ep"), None),
            P("tp", None),
            P("ep", None, "tp"),
            P("ep", None, "tp"),
            P("ep", "tp", None),
            P("tp", None),
        ),
        out_specs=P(("groups", "ep"), "tp"),
        check_vma=False,
    )
```

```python
import functools

import jax
import jax.numpy as jnp
from jax import lax
from jax.experimental import pallas as pl
from jax.experimental.pallas import tpu as pltpu
from jax.sharding import PartitionSpec as P

F32, BF16 = jnp.float32, jnp.bfloat16
MESH = pl.DeviceIdType.MESH
SLOTS = 4


def remote(src, dst, send, recv, **where):
    return pltpu.make_async_remote_copy(
        src_ref=src, dst_ref=dst, send_sem=send, recv_sem=recv, device_id=where, device_id_type=MESH
    )


def layer(
    ep_n, tp_n, tok_ref, pack_ref, wl_ref, wg_hbm, wu_hbm, wo_hbm, wr_hbm, out_ref,
    p_send, p_recv, lat, pack, wg, wu, wo, wr, acc, r1_send, r1_recv, r2_send, r2_recv,
    r3_send, r3_recv, comb,
    p_sems, k_sems, a_sems, b1_sems, b2_sems, b3_sems, w_sems, wr_sems, own_sem,
    r1_sems, r2_sems, r3_sems, c_sems,
):
    ep, tp = lax.axis_index("ep"), lax.axis_index("tp")
    far = lax.rem(tp + 2, 4)
    near = tp + 1 - 2 * lax.rem(tp, 2)
    near_far = lax.rem(near + 2, 4)
    count = wg_hbm.shape[0]
    slots = wg.shape[0]
    toks, top = tok_ref.shape[0], pack_ref.shape[1] // 2
    rows, width = lat.shape
    quarter = width // tp_n
    out_cols = out_ref.shape[1]

    def cols(q):
        return pl.ds(pl.multiple_of(q * quarter, quarter), quarter)

    def block(b):
        return pl.ds(pl.multiple_of(b * toks, toks), toks)

    def loads(e, s):
        return [
            pltpu.make_async_copy(hbm.at[e], vmem.at[s], w_sems.at[s, i])
            for i, (hbm, vmem) in enumerate(((wg_hbm, wg), (wu_hbm, wu), (wo_hbm, wo)))
        ]

    for s in range(slots):
        for c in loads(s, s):
            c.start()

    barrier = pltpu.get_barrier_semaphore()
    for d in range(1, ep_n):
        pl.semaphore_signal(barrier, inc=1, device_id={"ep": lax.rem(ep + d, ep_n)}, device_id_type=MESH)
    for d in range(1, tp_n):
        pl.semaphore_signal(barrier, inc=1, device_id={"tp": lax.rem(tp + d, tp_n)}, device_id_type=MESH)
    pl.semaphore_wait(barrier, ep_n + tp_n - 2)

    sent = []

    parts = [None]
    for d in range(1, tp_n):
        peer = lax.rem(tp + d, tp_n)
        p_send[d] = jnp.dot(tok_ref[...], wl_ref[:, cols(peer)], preferred_element_type=F32).astype(BF16)
        c = remote(p_send.at[d], p_recv.at[d], p_sems.at[0, d], p_sems.at[1, d], tp=peer)
        c.start()
        parts.append(c)
        sent.append(c)
    mine = jnp.dot(tok_ref[...], wl_ref[:, cols(tp)], preferred_element_type=F32)
    packs = [None]
    pack[block(ep), :] = pack_ref[...]
    for d in range(1, ep_n):
        c = remote(
            pack_ref, pack.at[block(ep), :], k_sems.at[0, d], k_sems.at[1, d], ep=lax.rem(ep + d, ep_n)
        )
        c.start()
        packs.append(c)
        sent.append(c)
    for d in range(1, tp_n):
        parts[d].wait_recv()
        mine = mine + p_recv[d].astype(F32)
    lat[block(ep), cols(tp)] = mine.astype(BF16)

    own = lat.at[block(ep), cols(tp)]
    spread = [None]
    for d in range(1, ep_n):
        c = remote(own, own, a_sems.at[0, d], a_sems.at[1, d], ep=lax.rem(ep + d, ep_n))
        c.start()
        spread.append(c)
        sent.append(c)
    b1, b2, b3 = [], [], []
    for d in range(ep_n):
        if d:
            spread[d].wait_recv()
        piece = lat.at[block(lax.rem(ep + ep_n - d, ep_n)), cols(tp)]
        c = remote(piece, piece, b1_sems.at[0, d], b1_sems.at[1, d], tp=far)
        c.start()
        b1.append(c)
        c = remote(piece, piece, b2_sems.at[0, d], b2_sems.at[1, d], tp=near)
        c.start()
        b2.append(c)
    for d in range(ep_n):
        b1[d].wait_recv()
        piece = lat.at[block(lax.rem(ep + ep_n - d, ep_n)), cols(far)]
        c = remote(piece, piece, b3_sems.at[0, d], b3_sems.at[1, d], tp=near)
        c.start()
        b3.append(c)
    sent += b1 + b2 + b3
    for d in range(ep_n):
        b2[d].wait_recv()
        b3[d].wait_recv()
        if d:
            packs[d].wait_recv()

    restore = []
    for d in range(1, tp_n):
        peer = lax.rem(tp + d, tp_n)
        c = remote(
            wr_hbm.at[:, pl.ds(pl.multiple_of(peer * out_cols, out_cols), out_cols)],
            wr.at[cols(tp), :], wr_sems.at[0, d], wr_sems.at[1, d], tp=peer,
        )
        c.start()
        restore.append(c)
        sent.append(c)
    own_restore = pltpu.make_async_copy(
        wr_hbm.at[:, pl.ds(pl.multiple_of(tp * out_cols, out_cols), out_cols)], wr.at[cols(tp), :], own_sem
    )
    own_restore.start()

    acc[...] = jnp.zeros_like(acc)
    tile = min(rows, 512)
    hidden = wg.shape[2]
    strip = hidden // 2

    def expert(e, carry):
        s = lax.rem(e, slots)
        for c in loads(e, s):
            c.wait()
        name = (ep * count + e).astype(F32)

        def tiles(i, inner):
            r = pl.ds(pl.multiple_of(i * tile, tile), tile)
            x = lat[r, :]
            chosen = pack[r, :]
            weight = jnp.sum(
                jnp.where(chosen[:, :top] == name, chosen[:, top:], 0.0), axis=1, keepdims=True
            )
            hs = []
            for j in range(2):
                cut = pl.ds(j * strip, strip)
                g = jnp.dot(x, wg[s, :, cut], preferred_element_type=F32)
                u = jnp.dot(x, wu[s, :, cut], preferred_element_type=F32)
                hs.append((g / (1.0 + jnp.exp(-g)) * u * weight).astype(BF16))
            h = jnp.concatenate(hs, axis=1)
            acc[r, :] += jnp.dot(h, wo[s], preferred_element_type=F32)
            return inner

        if rows == tile:
            tiles(0, 0)
        else:
            lax.fori_loop(0, rows // tile, tiles, 0)

        @pl.when(e + slots < count)
        def _():
            for c in loads(e + slots, s):
                c.start()

        return carry

    lax.fori_loop(0, count, expert, 0)

    order = list(range(1, ep_n)) + [0]
    at = [block(lax.rem(ep + d, ep_n)) for d in range(ep_n)]
    r1, r2, r3 = {}, {}, {}
    for d in order:
        r1_send[d, 0] = acc[at[d], cols(near)].astype(BF16)
        r1_send[d, 1] = acc[at[d], cols(near_far)].astype(BF16)
        r1[d] = remote(r1_send.at[d], r1_recv.at[d], r1_sems.at[0, d], r1_sems.at[1, d], tp=near)
        r1[d].start()
    for d in order:
        r1[d].wait_recv()
        r2_send[d] = (acc[at[d], cols(far)] + r1_recv[d, 1].astype(F32)).astype(BF16)
        r2[d] = remote(r2_send.at[d], r2_recv.at[d], r2_sems.at[0, d], r2_sems.at[1, d], tp=far)
        r2[d].start()
    for d in order:
        r2[d].wait_recv()
        total = acc[at[d], cols(tp)] + r1_recv[d, 0].astype(F32) + r2_recv[d].astype(F32)
        if d:
            r3_send[d] = total.astype(BF16)
            r3[d] = remote(
                r3_send.at[d], r3_recv.at[d], r3_sems.at[0, d], r3_sems.at[1, d], ep=lax.rem(ep + d, ep_n)
            )
            r3[d].start()
    for d in range(1, ep_n):
        r3[d].wait_recv()
        total = total + r3_recv[d].astype(F32)
    sent += list(r1.values()) + list(r2.values()) + list(r3.values())
    comb[:, cols(tp)] = total.astype(BF16)
    gathered = []
    for d in range(1, tp_n):
        c = remote(
            comb.at[:, cols(tp)], comb.at[:, cols(tp)], c_sems.at[0, d], c_sems.at[1, d],
            tp=lax.rem(tp + d, tp_n),
        )
        c.start()
        gathered.append(c)
    sent += gathered
    own_restore.wait()
    for c in restore:
        c.wait_recv()
    for c in gathered:
        c.wait_recv()
    out_ref[...] = jnp.dot(comb[...], wr[...], preferred_element_type=F32).astype(out_ref.dtype)
    for c in sent:
        c.wait_send()


def solution(mesh):
    ep_n, tp_n = mesh.shape["ep"], mesh.shape["tp"]

    def shards(tokens, routes, gates, w_latent, w_gate, w_up, w_out, w_restore):
        toks = tokens.shape[0]
        count, width, hidden = w_gate.shape
        rows, quarter = toks * ep_n, width // tp_n
        out_cols = w_restore.shape[1] // tp_n
        slots = min(SLOTS, count)
        pack = jnp.concatenate([routes.astype(F32), gates], axis=1)
        vmem, dma = pltpu.VMEM, pltpu.SemaphoreType.DMA
        in_vmem, in_hbm = pl.BlockSpec(memory_space=pltpu.VMEM), pl.BlockSpec(memory_space=pl.ANY)
        work = 6 * rows * width * hidden * count
        return pl.pallas_call(
            functools.partial(layer, ep_n, tp_n),
            out_shape=jax.ShapeDtypeStruct((toks, out_cols), BF16),
            in_specs=[in_vmem] * 3 + [in_hbm] * 4,
            out_specs=in_vmem,
            scratch_shapes=[
                vmem((tp_n, toks, quarter), BF16),
                vmem((tp_n, toks, quarter), BF16),
                vmem((rows, width), BF16),
                vmem((rows, pack.shape[1]), F32),
                vmem((slots, width, hidden), BF16),
                vmem((slots, width, hidden), BF16),
                vmem((slots, hidden, width), BF16),
                vmem((width, out_cols), BF16),
                vmem((rows, width), F32),
                vmem((ep_n, 2, toks, quarter), BF16),
                vmem((ep_n, 2, toks, quarter), BF16),
                vmem((ep_n, toks, quarter), BF16),
                vmem((ep_n, toks, quarter), BF16),
                vmem((ep_n, toks, quarter), BF16),
                vmem((ep_n, toks, quarter), BF16),
                vmem((toks, width), BF16),
                dma((2, tp_n)),
                dma((2, ep_n)),
                dma((2, ep_n)),
                dma((2, ep_n)),
                dma((2, ep_n)),
                dma((2, ep_n)),
                dma((slots, 3)),
                dma((2, tp_n)),
                dma,
                dma((2, ep_n)),
                dma((2, ep_n)),
                dma((2, ep_n)),
                dma((2, tp_n)),
            ],
            compiler_params=pltpu.CompilerParams(
                collective_id=0, has_side_effects=True, vmem_limit_bytes=60 * 1024 * 1024
            ),
            cost_estimate=pl.CostEstimate(flops=work, bytes_accessed=6 * width * hidden * count, transcendentals=0),
        )(tokens, pack, w_latent, w_gate, w_up, w_out, w_restore)

    return jax.shard_map(
        shards,
        mesh=mesh,
        in_specs=(
            P(("groups", "ep"), "tp"),
            P(("groups", "ep"), None),
            P(("groups", "ep"), None),
            P("tp", None),
            P("ep", None, "tp"),
            P("ep", None, "tp"),
            P("ep", "tp", None),
            P("tp", None),
        ),
        out_specs=P(("groups", "ep"), "tp"),
        check_vma=False,
    )
```

```python
import functools

import jax
import jax.numpy as jnp
from jax import lax
from jax.experimental import pallas as pl
from jax.experimental.pallas import tpu as pltpu
from jax.sharding import PartitionSpec as P

F32, BF16 = jnp.float32, jnp.bfloat16
MESH = pl.DeviceIdType.MESH
SLOTS = 4


def remote(src, dst, send, recv, **where):
    return pltpu.make_async_remote_copy(
        src_ref=src, dst_ref=dst, send_sem=send, recv_sem=recv, device_id=where, device_id_type=MESH
    )


def layer(
    ep_n, tp_n, tok_ref, routes_ref, gates_ref, wl_ref, wg_hbm, wu_hbm, wo_hbm, wr_hbm, out_ref,
    p_send, p_recv, lat, pack, wg, wu, wo, wr, acc, r1_send, r1_recv, r2_send, r2_recv,
    r3_send, r3_recv, comb,
    p_sems, k_sems, a_sems, b1_sems, b2_sems, b3_sems, w_sems, wr_sems, own_sem,
    r1_sems, r2_sems, r3_sems, c_sems,
):
    ep, tp = lax.axis_index("ep"), lax.axis_index("tp")
    far = lax.rem(tp + 2, 4)
    near = tp + 1 - 2 * lax.rem(tp, 2)
    near_far = lax.rem(near + 2, 4)
    count = wg_hbm.shape[0]
    slots = wg.shape[0]
    toks, top = tok_ref.shape[0], routes_ref.shape[0]
    rows, width = lat.shape
    quarter = width // tp_n
    out_cols = out_ref.shape[1]

    def cols(q):
        return pl.ds(pl.multiple_of(q * quarter, quarter), quarter)

    def block(b):
        return pl.ds(pl.multiple_of(b * toks, toks), toks)

    def loads(e, s):
        return [
            pltpu.make_async_copy(hbm.at[e], vmem.at[s], w_sems.at[s, i])
            for i, (hbm, vmem) in enumerate(((wg_hbm, wg), (wu_hbm, wu), (wo_hbm, wo)))
        ]

    for s in range(slots):
        for c in loads(s, s):
            c.start()

    barrier = pltpu.get_barrier_semaphore()
    for d in range(1, ep_n):
        pl.semaphore_signal(barrier, inc=1, device_id={"ep": lax.rem(ep + d, ep_n)}, device_id_type=MESH)
    for d in range(1, tp_n):
        pl.semaphore_signal(barrier, inc=1, device_id={"tp": lax.rem(tp + d, tp_n)}, device_id_type=MESH)
    pl.semaphore_wait(barrier, ep_n + tp_n - 2)

    sent = []

    parts = [None]
    for d in range(1, tp_n):
        peer = lax.rem(tp + d, tp_n)
        p_send[d] = jnp.dot(tok_ref[...], wl_ref[:, cols(peer)], preferred_element_type=F32).astype(BF16)
        c = remote(p_send.at[d], p_recv.at[d], p_sems.at[0, d], p_sems.at[1, d], tp=peer)
        c.start()
        parts.append(c)
        sent.append(c)
    mine = jnp.dot(tok_ref[...], wl_ref[:, cols(tp)], preferred_element_type=F32)
    packs = [None]
    fill = jnp.zeros((pack.shape[1] - 2 * top, toks), F32)
    pack[block(ep), :] = jnp.concatenate([routes_ref[...].astype(F32), gates_ref[...], fill], axis=0).T
    for d in range(1, ep_n):
        c = remote(
            pack.at[block(ep), :], pack.at[block(ep), :], k_sems.at[0, d], k_sems.at[1, d], ep=lax.rem(ep + d, ep_n)
        )
        c.start()
        packs.append(c)
        sent.append(c)
    for d in range(1, tp_n):
        parts[d].wait_recv()
        mine = mine + p_recv[d].astype(F32)
    lat[block(ep), cols(tp)] = mine.astype(BF16)

    own = lat.at[block(ep), cols(tp)]
    spread = [None]
    for d in range(1, ep_n):
        c = remote(own, own, a_sems.at[0, d], a_sems.at[1, d], ep=lax.rem(ep + d, ep_n))
        c.start()
        spread.append(c)
        sent.append(c)
    b1, b2, b3 = [], [], []
    for d in range(ep_n):
        if d:
            spread[d].wait_recv()
        piece = lat.at[block(lax.rem(ep + ep_n - d, ep_n)), cols(tp)]
        c = remote(piece, piece, b1_sems.at[0, d], b1_sems.at[1, d], tp=far)
        c.start()
        b1.append(c)
        c = remote(piece, piece, b2_sems.at[0, d], b2_sems.at[1, d], tp=near)
        c.start()
        b2.append(c)
    for d in range(ep_n):
        b1[d].wait_recv()
        piece = lat.at[block(lax.rem(ep + ep_n - d, ep_n)), cols(far)]
        c = remote(piece, piece, b3_sems.at[0, d], b3_sems.at[1, d], tp=near)
        c.start()
        b3.append(c)
    sent += b1 + b2 + b3
    for d in range(ep_n):
        b2[d].wait_recv()
        b3[d].wait_recv()
        if d:
            packs[d].wait_recv()

    restore = []
    for d in range(1, tp_n):
        peer = lax.rem(tp + d, tp_n)
        c = remote(
            wr_hbm.at[:, pl.ds(pl.multiple_of(peer * out_cols, out_cols), out_cols)],
            wr.at[cols(tp), :], wr_sems.at[0, d], wr_sems.at[1, d], tp=peer,
        )
        c.start()
        restore.append(c)
        sent.append(c)
    own_restore = pltpu.make_async_copy(
        wr_hbm.at[:, pl.ds(pl.multiple_of(tp * out_cols, out_cols), out_cols)], wr.at[cols(tp), :], own_sem
    )
    own_restore.start()

    acc[...] = jnp.zeros_like(acc)
    tile = min(rows, 512)
    hidden = wg.shape[2]
    strip = hidden // 2

    def expert(e, carry):
        s = lax.rem(e, slots)
        for c in loads(e, s):
            c.wait()
        name = (ep * count + e).astype(F32)

        def tiles(i, inner):
            r = pl.ds(pl.multiple_of(i * tile, tile), tile)
            x = lat[r, :]
            chosen = pack[r, :]
            weight = jnp.sum(
                jnp.where(chosen[:, :top] == name, chosen[:, top : 2 * top], 0.0), axis=1, keepdims=True
            )
            hs = []
            for j in range(2):
                cut = pl.ds(j * strip, strip)
                g = jnp.dot(x, wg[s, :, cut], preferred_element_type=F32)
                u = jnp.dot(x, wu[s, :, cut], preferred_element_type=F32)
                hs.append((g / (1.0 + jnp.exp(-g)) * u * weight).astype(BF16))
            h = jnp.concatenate(hs, axis=1)
            acc[r, :] += jnp.dot(h, wo[s], preferred_element_type=F32)
            return inner

        if rows == tile:
            tiles(0, 0)
        else:
            lax.fori_loop(0, rows // tile, tiles, 0)

        @pl.when(e + slots < count)
        def _():
            for c in loads(e + slots, s):
                c.start()

        return carry

    lax.fori_loop(0, count, expert, 0)

    order = list(range(1, ep_n)) + [0]
    at = [block(lax.rem(ep + d, ep_n)) for d in range(ep_n)]
    r1, r2, r3 = {}, {}, {}
    for d in order:
        r1_send[d, 0] = acc[at[d], cols(near)].astype(BF16)
        r1_send[d, 1] = acc[at[d], cols(near_far)].astype(BF16)
        r1[d] = remote(r1_send.at[d], r1_recv.at[d], r1_sems.at[0, d], r1_sems.at[1, d], tp=near)
        r1[d].start()
    for d in order:
        r1[d].wait_recv()
        r2_send[d] = (acc[at[d], cols(far)] + r1_recv[d, 1].astype(F32)).astype(BF16)
        r2[d] = remote(r2_send.at[d], r2_recv.at[d], r2_sems.at[0, d], r2_sems.at[1, d], tp=far)
        r2[d].start()
    for d in order:
        r2[d].wait_recv()
        total = acc[at[d], cols(tp)] + r1_recv[d, 0].astype(F32) + r2_recv[d].astype(F32)
        if d:
            r3_send[d] = total.astype(BF16)
            r3[d] = remote(
                r3_send.at[d], r3_recv.at[d], r3_sems.at[0, d], r3_sems.at[1, d], ep=lax.rem(ep + d, ep_n)
            )
            r3[d].start()
    for d in range(1, ep_n):
        r3[d].wait_recv()
        total = total + r3_recv[d].astype(F32)
    sent += list(r1.values()) + list(r2.values()) + list(r3.values())
    comb[:, cols(tp)] = total.astype(BF16)
    gathered = []
    for d in range(1, tp_n):
        c = remote(
            comb.at[:, cols(tp)], comb.at[:, cols(tp)], c_sems.at[0, d], c_sems.at[1, d],
            tp=lax.rem(tp + d, tp_n),
        )
        c.start()
        gathered.append(c)
    sent += gathered
    own_restore.wait()
    for c in restore:
        c.wait_recv()
    result = jnp.dot(comb[:, cols(tp)], wr[cols(tp), :], preferred_element_type=F32)
    for d in range(1, tp_n):
        gathered[d - 1].wait_recv()
        peer = lax.rem(tp + tp_n - d, tp_n)
        result = result + jnp.dot(comb[:, cols(peer)], wr[cols(peer), :], preferred_element_type=F32)
    out_ref[...] = result.astype(out_ref.dtype)
    for c in sent:
        c.wait_send()


def solution(mesh):
    ep_n, tp_n = mesh.shape["ep"], mesh.shape["tp"]

    def shards(tokens, routes, gates, w_latent, w_gate, w_up, w_out, w_restore):
        toks = tokens.shape[0]
        count, width, hidden = w_gate.shape
        rows, quarter = toks * ep_n, width // tp_n
        out_cols = w_restore.shape[1] // tp_n
        slots = min(SLOTS, count)
        lanes = -(-2 * routes.shape[1] // 128) * 128
        vmem, dma = pltpu.VMEM, pltpu.SemaphoreType.DMA
        in_vmem, in_hbm = pl.BlockSpec(memory_space=pltpu.VMEM), pl.BlockSpec(memory_space=pl.ANY)
        work = 6 * rows * width * hidden * count
        return pl.pallas_call(
            functools.partial(layer, ep_n, tp_n),
            out_shape=jax.ShapeDtypeStruct((toks, out_cols), BF16),
            in_specs=[in_vmem] * 4 + [in_hbm] * 4,
            out_specs=in_vmem,
            scratch_shapes=[
                vmem((tp_n, toks, quarter), BF16),
                vmem((tp_n, toks, quarter), BF16),
                vmem((rows, width), BF16),
                vmem((rows, lanes), F32),
                vmem((slots, width, hidden), BF16),
                vmem((slots, width, hidden), BF16),
                vmem((slots, hidden, width), BF16),
                vmem((width, out_cols), BF16),
                vmem((rows, width), F32),
                vmem((ep_n, 2, toks, quarter), BF16),
                vmem((ep_n, 2, toks, quarter), BF16),
                vmem((ep_n, toks, quarter), BF16),
                vmem((ep_n, toks, quarter), BF16),
                vmem((ep_n, toks, quarter), BF16),
                vmem((ep_n, toks, quarter), BF16),
                vmem((toks, width), BF16),
                dma((2, tp_n)),
                dma((2, ep_n)),
                dma((2, ep_n)),
                dma((2, ep_n)),
                dma((2, ep_n)),
                dma((2, ep_n)),
                dma((slots, 3)),
                dma((2, tp_n)),
                dma,
                dma((2, ep_n)),
                dma((2, ep_n)),
                dma((2, ep_n)),
                dma((2, tp_n)),
            ],
            compiler_params=pltpu.CompilerParams(
                collective_id=0, has_side_effects=True, vmem_limit_bytes=60 * 1024 * 1024
            ),
            cost_estimate=pl.CostEstimate(flops=work, bytes_accessed=6 * width * hidden * count, transcendentals=0),
        )(tokens, routes.T, gates.T, w_latent, w_gate, w_up, w_out, w_restore)

    return jax.shard_map(
        shards,
        mesh=mesh,
        in_specs=(
            P(("groups", "ep"), "tp"),
            P(("groups", "ep"), None),
            P(("groups", "ep"), None),
            P("tp", None),
            P("ep", None, "tp"),
            P("ep", None, "tp"),
            P("ep", "tp", None),
            P("tp", None),
        ),
        out_specs=P(("groups", "ep"), "tp"),
        check_vma=False,
    )
```
